32 devices in a mesh: rep: 2 (over y), tp: 8 (over z, x), sp: 2 (over core).
Axes of the slice: x: 2, y: 2, z: 4, core: 2. Of those that a mesh axis runs over, the one named last changes fastest.
Arguments:
- tokens: bfloat16 [2048, 8192], P(('rep', 'sp'), 'tp'), parts along dimension 0
- norm_gain_vector: bfloat16 [8192], P('tp'), may hold values from 0.099609375 to 1.8984375
- gate_weight: bfloat16 [8192, 16384], P(None, 'tp'), may hold values from -0.0625 to 0.0625
- up_weight: bfloat16 [8192, 16384], P(None, 'tp'), may hold values from -0.0625 to 0.0625
- adapter_down_maps: bfloat16 [32, 8192, 32], P(None, 'tp'), may hold values from -0.0625 to 0.0625
- adapter_up_maps: bfloat16 [2, 32, 16, 16384], P(None, None, None, 'tp'), may hold values from -0.75 to 0.75
- adapter_of_row: int32 [2048], P(('rep', 'sp')), parts along dimension 0, may hold values from 0 to 31, as said below
- adapter_first_rows: int32 [64], P('rep'), parts along dimension 0, may hold values from 0 to 1023, as said below
- adapter_row_counts: int32 [64], P('rep'), parts along dimension 0, may hold values from 1 to 63, as said below
Outputs:
- hidden: bfloat16 [2048, 16384], P(('rep', 'sp'), 'tp'), parts along dimension 0
The draws below stay inside these ranges and needn't reach their ends.
There are 2 independent parts, one for each index of `rep`. The reference program is written for one: setup_inputs(seed, part) draws one part's arguments, and reference() takes and returns one part's arrays. A program takes and returns all parts, laid end to end along the dimension named above; an argument that names none is the same for every part. Nothing has to cross between parts.
Inputs may be any that keep to these rules, and one draw needn't show every extreme that they name: Rows are grouped by adapter: adapter_of_row does not decrease from one row to the next, and every adapter has at least one row. adapter_first_rows[a] is the number of rows whose adapter is below a. adapter_row_counts[a] is the number of rows whose adapter is a; they sum to 1024.
All inputs are finite; a program needn't handle non-finite values.
Results may differ from the reference program's by a relative error of at most 0.0061.
Values may be sent and summed in bfloat16 or wider, within the bound.
A program may use at most 192 MiB of HBM per device.

```python
import math
import jax
import jax.numpy as jnp
from jax import lax

MODEL_WIDTH = 8192
HIDDEN_UNITS = 16384
ADAPTER_RANK = 16
ADAPTER_COUNT = 32
TOKEN_COUNT = 1024


def adapter_layout(key):
    offset_key = jax.random.fold_in(key, 101)
    pick_key = jax.random.fold_in(key, 202)
    base_rows = TOKEN_COUNT // ADAPTER_COUNT
    pair_count = ADAPTER_COUNT // 2
    offsets = jax.random.randint(offset_key, (pair_count,), 1 - base_rows, base_rows)
    forced = jax.random.randint(pick_key, (), 0, pair_count)
    pair_range = jnp.arange(pair_count, dtype=jnp.int32)
    offsets = jnp.where(pair_range == forced, base_rows - 1, offsets)
    counts = jnp.stack([base_rows + offsets, base_rows - offsets], axis=1).reshape(ADAPTER_COUNT)
    return counts.astype(jnp.int32)


def draw_adapter_row_counts(key, part):
    return adapter_layout(key)


def draw_adapter_first_rows(key, part):
    counts = adapter_layout(key)
    return (jnp.cumsum(counts) - counts).astype(jnp.int32)


def draw_adapter_of_row(key, part):
    counts = adapter_layout(key)
    ends = jnp.cumsum(counts)
    row_index = jnp.arange(TOKEN_COUNT, dtype=jnp.int32)
    return jnp.sum((ends[None, :] <= row_index[:, None]).astype(jnp.int32), axis=1).astype(jnp.int32)


def draw_tokens(key, part):
    key = jax.random.fold_in(key, 11)
    base_key = jax.random.fold_in(key, 1)
    row_key = jax.random.fold_in(key, 2)
    col_key = jax.random.fold_in(key, 3)
    base = jax.random.normal(base_key, (TOKEN_COUNT, MODEL_WIDTH), jnp.float32)
    row_scale = jnp.exp(jax.random.uniform(row_key, (TOKEN_COUNT, 1), jnp.float32, 0.0, math.log(10.0)))
    rising = math.log(3.0) * jnp.arange(MODEL_WIDTH, dtype=jnp.float32)[None, :] / MODEL_WIDTH
    col_scale = jnp.exp(rising + jax.random.uniform(col_key, (1, MODEL_WIDTH), jnp.float32, 0.0, math.log(3.3)))
    return (0.25 * base * row_scale * col_scale).astype(jnp.bfloat16)


def block_scale(rng, dims, shards, least, largest):
    def one(dim, shards_of):
        steps = jax.random.uniform(jax.random.fold_in(jax.random.fold_in(rng, 6), dim), (shards_of,), jnp.float32, least / len(shards), largest / len(shards))
        return jnp.repeat(jnp.exp(steps), dims[dim] // shards_of).reshape((-1,) + (1,) * (len(dims) - dim - 1))

    loudness = one(*shards[0])
    for cut in shards[1:]:
        loudness = loudness * one(*cut)
    return loudness


def noise(rng, dims, scale, most, cuts=(), kind=jnp.bfloat16):
    gain = block_scale(rng, dims, cuts, -0.22, 0.18) if cuts else 1.0
    values = jax.random.normal(rng, dims, jnp.float32) * scale * gain
    return jnp.minimum(jnp.maximum(values, -most), most).astype(kind)


def setup_inputs(seed: int = 0, part: int = 0) -> dict:
    key_of = jax.random.split(jax.random.key(seed), 10)
    own_keys = jax.random.split(jax.random.fold_in(key_of[9], part), 10)
    tokens = draw_tokens(jax.random.fold_in(jax.random.fold_in(key_of[9], part), 71), part)
    norm_gain_vector = jnp.clip(1.0 + 0.18 * jax.random.normal(key_of[1], (MODEL_WIDTH,), jnp.float32), 0.099609375, 1.8984375).astype(jnp.bfloat16)
    gate_weight = noise(key_of[2], (MODEL_WIDTH, HIDDEN_UNITS), MODEL_WIDTH ** -0.5, 0.0625, ((1, 8),))
    up_weight = noise(key_of[3], (MODEL_WIDTH, HIDDEN_UNITS), MODEL_WIDTH ** -0.5, 0.0625, ((1, 8),))
    adapter_down_maps = noise(key_of[4], (ADAPTER_COUNT, MODEL_WIDTH, 2 * ADAPTER_RANK), MODEL_WIDTH ** -0.5, 0.0625, ((1, 8),))
    adapter_up_maps = noise(key_of[5], (2, ADAPTER_COUNT, ADAPTER_RANK, HIDDEN_UNITS), (4 * ADAPTER_RANK) ** -0.5, 0.75, ((3, 8),))
    adapter_of_row = draw_adapter_of_row(jax.random.fold_in(jax.random.fold_in(key_of[9], part), 71), part)
    adapter_first_rows = draw_adapter_first_rows(jax.random.fold_in(jax.random.fold_in(key_of[9], part), 71), part)
    adapter_row_counts = draw_adapter_row_counts(jax.random.fold_in(jax.random.fold_in(key_of[9], part), 71), part)
    return {"tokens": tokens, "norm_gain_vector": norm_gain_vector, "gate_weight": gate_weight, "up_weight": up_weight, "adapter_down_maps": adapter_down_maps, "adapter_up_maps": adapter_up_maps, "adapter_of_row": adapter_of_row, "adapter_first_rows": adapter_first_rows, "adapter_row_counts": adapter_row_counts}


epsilon = 1e-05

def reference(tokens, norm_gain_vector, gate_weight, up_weight, adapter_down_maps, adapter_up_maps, adapter_of_row, adapter_first_rows, adapter_row_counts):
    values = tokens.astype(jnp.float32)
    gain_vec = norm_gain_vector.astype(jnp.float32)
    inverse = lax.rsqrt(lax.optimization_barrier(jnp.sum(values * values, axis=1, keepdims=True)) / MODEL_WIDTH + epsilon)
    normed_input = (values * inverse * gain_vec).astype(jnp.bfloat16)
    scaled_input = (values * gain_vec).astype(jnp.bfloat16)
    adapter_flattened = jnp.transpose(adapter_down_maps, (1, 0, 2)).reshape(MODEL_WIDTH, ADAPTER_COUNT * 2 * ADAPTER_RANK)
    combined_terms = jnp.dot(scaled_input, adapter_flattened, preferred_element_type=jnp.float32).reshape(TOKEN_COUNT, ADAPTER_COUNT, 2 * ADAPTER_RANK)
    adapter_range = jnp.arange(ADAPTER_COUNT, dtype=jnp.int32)
    selector = (adapter_of_row[:, None] == adapter_range[None, :]).astype(jnp.float32)
    shrink = (inverse * lax.optimization_barrier(jnp.sum(selector[:, :, None] * combined_terms, axis=1))).astype(jnp.bfloat16)
    row_index = jnp.arange(TOKEN_COUNT, dtype=jnp.int32)[:, None]
    member = ((row_index >= adapter_first_rows[None, :]) & (row_index < (adapter_first_rows + adapter_row_counts)[None, :])).astype(jnp.bfloat16)
    raised_gate = (member[:, :, None] * shrink[:, None, :ADAPTER_RANK]).reshape(TOKEN_COUNT, ADAPTER_COUNT * ADAPTER_RANK)
    raised_up = (member[:, :, None] * shrink[:, None, ADAPTER_RANK:]).reshape(TOKEN_COUNT, ADAPTER_COUNT * ADAPTER_RANK)
    gate_output = jnp.dot(normed_input, gate_weight, preferred_element_type=jnp.float32) + jnp.dot(raised_gate, adapter_up_maps[0].reshape(ADAPTER_COUNT * ADAPTER_RANK, HIDDEN_UNITS), preferred_element_type=jnp.float32)
    up_output = jnp.dot(normed_input, up_weight, preferred_element_type=jnp.float32) + jnp.dot(raised_up, adapter_up_maps[1].reshape(ADAPTER_COUNT * ADAPTER_RANK, HIDDEN_UNITS), preferred_element_type=jnp.float32)
    return (jax.nn.silu(gate_output) * up_output).astype(jnp.bfloat16)
```

```python
import functools
import jax
import jax.numpy as jnp
from jax import lax
from jax.experimental import pallas as pl
from jax.experimental.pallas import tpu as pltpu
from jax.sharding import PartitionSpec as P

epsilon = 1e-05
MESH = pl.DeviceIdType.MESH
F32 = jnp.float32
BF16 = jnp.bfloat16


def rank_products(scaled_columns, adapter_slice, adapter_of_row):
    adapter_total, slice_width, rank_doubled = adapter_slice.shape
    adapter_flattened = jnp.transpose(adapter_slice, (1, 0, 2)).reshape(
        slice_width, adapter_total * rank_doubled
    )
    combined_terms = jnp.dot(scaled_columns, adapter_flattened, preferred_element_type=jnp.float32)
    combined_terms = combined_terms.reshape(scaled_columns.shape[0], adapter_total, rank_doubled)
    adapter_range = jnp.arange(adapter_total, dtype=jnp.int32)
    selector = (adapter_of_row[:, None] == adapter_range[None, :]).astype(jnp.float32)
    return jnp.sum(selector[:, :, None] * combined_terms, axis=1)


def local(
    tokens,
    norm_gain_vector,
    gate_weight,
    up_weight,
    adapter_down_maps,
    adapter_up_maps,
    adapter_of_row,
    adapter_first_rows,
    adapter_row_counts,
):
    rows_here = tokens.shape[0]
    total_width = tokens.shape[1] * lax.axis_size("tp")
    rank_single = adapter_up_maps.shape[2]
    adapter_total = adapter_up_maps.shape[1]
    values = tokens.astype(jnp.float32)
    gain_local = norm_gain_vector.astype(jnp.float32)
    scaled_input = (values * gain_local).astype(jnp.bfloat16)
    gathered, gain_all = (
        lax.all_gather(tokens, "tp", axis=1, tiled=True),
        lax.all_gather(norm_gain_vector, "tp", axis=0, tiled=True),
    )
    wide_values = gathered.astype(jnp.float32)
    inverse = lax.rsqrt(
        jnp.sum(wide_values * wide_values, axis=1, keepdims=True) / total_width + epsilon
    )
    normed_input = (wide_values * inverse * gain_all.astype(jnp.float32)).astype(jnp.bfloat16)
    gate_base = jnp.dot(normed_input, gate_weight, preferred_element_type=jnp.float32)
    up_base = jnp.dot(normed_input, up_weight, preferred_element_type=jnp.float32)
    partial_output = rank_products(scaled_input, adapter_down_maps, adapter_of_row)
    shrink = (inverse * lax.psum(partial_output, "tp")).astype(jnp.bfloat16)
    row_index = lax.axis_index("sp") * rows_here + jnp.arange(rows_here, dtype=jnp.int32)[:, None]
    member = (
        (row_index >= adapter_first_rows[None, :])
        & (row_index < (adapter_first_rows + adapter_row_counts)[None, :])
    ).astype(jnp.bfloat16)
    raised_gate = (member[:, :, None] * shrink[:, None, :rank_single]).reshape(
        rows_here, adapter_total * rank_single
    )
    raised_up = (member[:, :, None] * shrink[:, None, rank_single:]).reshape(
        rows_here, adapter_total * rank_single
    )
    column_slice = adapter_up_maps.shape[3]
    gate_output = gate_base + jnp.dot(
        raised_gate,
        adapter_up_maps[0].reshape(adapter_total * rank_single, column_slice),
        preferred_element_type=jnp.float32,
    )
    up_output = up_base + jnp.dot(
        raised_up,
        adapter_up_maps[1].reshape(adapter_total * rank_single, column_slice),
        preferred_element_type=jnp.float32,
    )
    return (jax.nn.silu(gate_output) * up_output).astype(jnp.bfloat16)


SLOTS = 4


def ring_kernel(
    n, ranks, adapters,
    tokens, gain, first, count, gate_w, up_w, down, raise_maps,
    out,
    own, held, acc, weights, down_v, raise_v, squares, sums, sums_in, raised, inverse,
    ring_send, ring_recv, sum_send, sum_recv, weight_sem, map_sem,
):
    rows, width = tokens.shape
    half = width // 2
    units = out.shape[1]
    last = n - 1
    levels = n.bit_length() - 1
    me = lax.axis_index("tp")
    side = me % 2
    place = me // 2 + side * (n - 1 - 2 * (me // 2))

    def device_at(p):
        upper = p // (n // 2)
        return (1 - upper) * 2 * p + upper * (2 * (n - 1 - p) + 1)

    sends_to = (device_at((place + 1) % n), device_at((place + n - 1) % n))

    def owner_of(d, k):
        distance = k // 2 + 1
        return device_at((place + n - distance) % n) if d == 0 else device_at((place + distance) % n)

    def half_of(d, k):
        return k % 2 if d == 0 else 1 - k % 2

    def ring_copy(d, k, src):
        return pltpu.make_async_remote_copy(
            src_ref=src, dst_ref=held.at[d, k],
            send_sem=ring_send.at[d, k], recv_sem=ring_recv.at[d, k],
            device_id={"tp": sends_to[d]}, device_id_type=MESH,
        )

    def sum_copy(level):
        step = 2 ** level
        partner = me + step * (1 - 2 * ((me // step) % 2))
        return pltpu.make_async_remote_copy(
            src_ref=sums.at[level], dst_ref=sums_in.at[level],
            send_sem=sum_send.at[level], recv_sem=sum_recv.at[level],
            device_id={"tp": partner}, device_id_type=MESH,
        )

    def weight_copies(slot, start):
        here = pl.ds(pl.multiple_of(start, half), half)
        return (
            pltpu.make_async_copy(gate_w.at[here, :], weights.at[slot, 0], weight_sem.at[slot, 0]),
            pltpu.make_async_copy(up_w.at[here, :], weights.at[slot, 1], weight_sem.at[slot, 1]),
        )

    def fetch(slot, start):
        for c in weight_copies(slot, start):
            c.start()

    def fetched(slot):
        for c in weight_copies(slot, 0):
            c.wait()

    def start_of(d, k):
        return owner_of(d, k) * width + half_of(d, k) * half

    down_copy = pltpu.make_async_copy(down, down_v, map_sem.at[0])
    raise_copy = pltpu.make_async_copy(raise_maps, raise_v, map_sem.at[1])
    down_copy.start()
    fetch(0, me * width)
    fetch(1, me * width + half)
    raise_copy.start()
    fetch(2, start_of(0, 0))

    barrier = pltpu.get_barrier_semaphore()
    for d in range(1, n):
        pl.semaphore_signal(barrier, inc=1, device_id={"tp": (me + d) % n}, device_id_type=MESH)

    gain_row = gain[...].astype(F32)
    scale_rows = 64

    @pl.loop(0, rows // scale_rows)
    def _(i):
        here = pl.ds(pl.multiple_of(i * scale_rows, scale_rows), scale_rows)
        values = tokens[here, :].astype(F32)
        scaled = (values * gain_row).astype(BF16)
        own[0, here, :] = scaled[:, :half]
        own[1, here, :] = scaled[:, half:]
        squared = values * values
        total = squared[:, :128]
        for j in range(1, width // 128):
            total = total + squared[:, j * 128:(j + 1) * 128]
        squares[here, :] = total

    pl.semaphore_wait(barrier, n - 1)
    for k in range(2):
        for d in range(2):
            ring_copy(d, k, own.at[half_of(d, k)]).start()

    row_index = lax.broadcasted_iota(jnp.int32, (1, rows), 1) + lax.axis_index("sp") * rows

    def member(a):
        return (row_index >= first[a]) & (row_index < first[a] + count[a])

    down_copy.wait()
    sums[0, 0:ranks, :] = jnp.zeros((ranks, rows), F32)
    group = 4

    @pl.loop(0, adapters // group)
    def _(i):
        here = pl.ds(pl.multiple_of(i * group * ranks, group * ranks), group * ranks)
        dims = (((1,), (1,)), ((), ()))
        terms = lax.dot_general(down_v[here, :half], own[0], dims, preferred_element_type=F32)
        terms = terms + lax.dot_general(down_v[here, half:], own[1], dims, preferred_element_type=F32)
        total = sums[0, 0:ranks, :]
        for j in range(group):
            total = total + jnp.where(member(i * group + j), terms[j * ranks:(j + 1) * ranks, :], 0.0)
        sums[0, 0:ranks, :] = total

    square_sum = jnp.sum(jnp.transpose(squares[...]), axis=0, keepdims=True)
    sums[0, ranks:ranks + 8, :] = jnp.broadcast_to(square_sum, (8, rows))
    sum_copy(0).start()

    tile = 512 if units % 512 == 0 else units

    def product(x, slot, w, here):
        return jnp.dot(x, weights[slot, w, :, here], preferred_element_type=F32)

    def tiles(body):
        @pl.loop(0, units // tile)
        def _(i):
            body(pl.ds(pl.multiple_of(i * tile, tile), tile))

    fetched(0)
    fetch(3, start_of(1, 0))
    fetched(1)

    def own_tile(here):
        for w in range(2):
            acc[w, :, here] = product(own[0], 0, w, here) + product(own[1], 1, w, here)

    tiles(own_tile)

    def arrive(k):
        for d in range(2):
            ring_copy(d, k, own.at[0]).wait_recv()

            @pl.when(k + 2 < last)
            def _():
                ring_copy(d, k + 2, held.at[d, k]).start()

    def slots_of(k):
        low = 2 * ((k + 1) % 2)
        return low, low + 1

    def prefetch(k):
        @pl.when(k + 1 < last)
        def _():
            low, high = slots_of(k + 1)
            fetch(low, start_of(0, k + 1))
            fetch(high, start_of(1, k + 1))

    def steps(low, high, scaled):
        def step(k, carry):
            prefetch(k)
            arrive(k)
            s0, s1 = slots_of(k)
            fetched(s0)
            fetched(s1)

            def body(here):
                for w in range(2):
                    term = product(held[0, k], s0, w, here) + product(held[1, k], s1, w, here)
                    if scaled:
                        term = term * inverse[:, 0:1]
                    acc[w, :, here] += term

            tiles(body)
            return carry

        lax.fori_loop(low, high, step, 0)

    for level in range(levels):
        steps(level, level + 1, False)
        sum_copy(level).wait()
        sums[level + 1] = sums[level] + sums_in[level]
        if level + 1 < levels:
            sum_copy(level + 1).start()

    inverse_row = lax.rsqrt(sums[levels, ranks:ranks + 1, :] / (width * n) + epsilon)
    shrink = (sums[levels, 0:ranks, :] * inverse_row).astype(BF16).astype(F32)
    inverse[...] = jnp.transpose(jnp.broadcast_to(inverse_row, (128, rows)))
    rank = ranks // 2

    for a in range(adapters):
        chosen = jnp.where(member(a), shrink, 0.0).astype(BF16)
        for w in range(2):
            raised[w, a * rank:(a + 1) * rank, :] = chosen[w * rank:(w + 1) * rank, :]
    raise_copy.wait()
    depth = adapters * rank

    def raise_tile(here):
        for w in range(2):
            term = lax.dot_general(
                raised[w], raise_v[w * depth:(w + 1) * depth, here],
                (((0,), (0,)), ((), ())), preferred_element_type=F32,
            )
            acc[w, :, here] = acc[w, :, here] * inverse[:, 0:1] + term

    tiles(raise_tile)

    steps(levels, last - 1, True)

    arrive(last - 1)
    s0, s1 = slots_of(last - 1)
    fetched(s0)
    fetched(s1)

    def final_tile(here):
        found = []
        for w in range(2):
            term = product(held[0, last - 1], s0, w, here) + product(held[1, last - 1], s1, w, here)
            found.append(acc[w, :, here] + term * inverse[:, 0:1])
        gate, up = found
        out[:, here] = (gate / (1.0 + jnp.exp(-gate)) * up).astype(out.dtype)

    tiles(final_tile)

    for d in range(2):
        for k in range(last):
            ring_copy(d, k, own.at[0]).wait_send()


def local_ring(
    n, tokens, norm_gain_vector, gate_weight, up_weight, adapter_down_maps, adapter_up_maps,
    adapter_of_row, adapter_first_rows, adapter_row_counts,
):
    rows, width = tokens.shape
    units = gate_weight.shape[1]
    adapters, _, ranks = adapter_down_maps.shape
    half = width // 2
    levels = n.bit_length() - 1
    down = jnp.transpose(adapter_down_maps, (0, 2, 1)).reshape(adapters * ranks, width)
    raise_maps = adapter_up_maps.reshape(adapters * ranks, units)
    vmem = pl.BlockSpec(memory_space=pltpu.VMEM)
    smem = pl.BlockSpec(memory_space=pltpu.SMEM)
    anywhere = pl.BlockSpec(memory_space=pl.ANY)
    dma = pltpu.SemaphoreType.DMA
    return pl.pallas_call(
        functools.partial(ring_kernel, n, ranks, adapters),
        out_shape=jax.ShapeDtypeStruct((rows, units), BF16),
        in_specs=[vmem, vmem, smem, smem, anywhere, anywhere, anywhere, anywhere],
        out_specs=vmem,
        scratch_shapes=[
            pltpu.VMEM((2, rows, half), BF16),
            pltpu.VMEM((2, n - 1, rows, half), BF16),
            pltpu.VMEM((2, rows, units), F32),
            pltpu.VMEM((SLOTS, 2, half, units), BF16),
            pltpu.VMEM((adapters * ranks, width), BF16),
            pltpu.VMEM((adapters * ranks, units), BF16),
            pltpu.VMEM((rows, 128), F32),
            pltpu.VMEM((levels + 1, ranks + 8, rows), F32),
            pltpu.VMEM((levels, ranks + 8, rows), F32),
            pltpu.VMEM((2, adapters * ranks // 2, rows), BF16),
            pltpu.VMEM((rows, 128), F32),
            dma((2, n - 1)),
            dma((2, n - 1)),
            dma((levels,)),
            dma((levels,)),
            dma((SLOTS, 2)),
            dma((2,)),
        ],
        compiler_params=pltpu.CompilerParams(
            collective_id=0, has_side_effects=True, vmem_limit_bytes=60 * 1024 * 1024
        ),
        cost_estimate=pl.CostEstimate(
            flops=4 * rows * width * n * units, bytes_accessed=4 * width * n * units,
            transcendentals=rows * units,
        ),
    )(
        tokens, norm_gain_vector.reshape(1, width), adapter_first_rows, adapter_row_counts,
        gate_weight, up_weight, down, raise_maps,
    )


def solution(mesh):
    placed = (
        P(("rep", "sp"), "tp"),
        P("tp"),
        P(None, "tp"),
        P(None, "tp"),
        P(None, "tp", None),
        P(None, None, None, "tp"),
        P(("rep", "sp")),
        P("rep"),
        P("rep"),
    )
    n = mesh.shape["tp"]

    def body(tokens, *others):
        ring = n % 2 == 0 and n & (n - 1) == 0 and 8 <= n <= 16 and tokens.shape[1] % 256 == 0
        if ring:
            return local_ring(n, tokens, *others)
        return local(tokens, *others)

    return jax.shard_map(
        body, mesh=mesh, in_specs=placed, out_specs=P(("rep", "sp"), "tp"), check_vma=False
    )
```

```python
import functools
import jax
import jax.numpy as jnp
from jax import lax
from jax.experimental import pallas as pl
from jax.experimental.pallas import tpu as pltpu
from jax.sharding import PartitionSpec as P

epsilon = 1e-05
MESH = pl.DeviceIdType.MESH
F32 = jnp.float32
BF16 = jnp.bfloat16


def rank_products(scaled_columns, adapter_slice, adapter_of_row):
    adapter_total, slice_width, rank_doubled = adapter_slice.shape
    adapter_flattened = jnp.transpose(adapter_slice, (1, 0, 2)).reshape(
        slice_width, adapter_total * rank_doubled
    )
    combined_terms = jnp.dot(scaled_columns, adapter_flattened, preferred_element_type=jnp.float32)
    combined_terms = combined_terms.reshape(scaled_columns.shape[0], adapter_total, rank_doubled)
    adapter_range = jnp.arange(adapter_total, dtype=jnp.int32)
    selector = (adapter_of_row[:, None] == adapter_range[None, :]).astype(jnp.float32)
    return jnp.sum(selector[:, :, None] * combined_terms, axis=1)


def local(
    tokens,
    norm_gain_vector,
    gate_weight,
    up_weight,
    adapter_down_maps,
    adapter_up_maps,
    adapter_of_row,
    adapter_first_rows,
    adapter_row_counts,
):
    rows_here = tokens.shape[0]
    total_width = tokens.shape[1] * lax.axis_size("tp")
    rank_single = adapter_up_maps.shape[2]
    adapter_total = adapter_up_maps.shape[1]
    values = tokens.astype(jnp.float32)
    gain_local = norm_gain_vector.astype(jnp.float32)
    scaled_input = (values * gain_local).astype(jnp.bfloat16)
    gathered, gain_all = (
        lax.all_gather(tokens, "tp", axis=1, tiled=True),
        lax.all_gather(norm_gain_vector, "tp", axis=0, tiled=True),
    )
    wide_values = gathered.astype(jnp.float32)
    inverse = lax.rsqrt(
        jnp.sum(wide_values * wide_values, axis=1, keepdims=True) / total_width + epsilon
    )
    normed_input = (wide_values * inverse * gain_all.astype(jnp.float32)).astype(jnp.bfloat16)
    gate_base = jnp.dot(normed_input, gate_weight, preferred_element_type=jnp.float32)
    up_base = jnp.dot(normed_input, up_weight, preferred_element_type=jnp.float32)
    partial_output = rank_products(scaled_input, adapter_down_maps, adapter_of_row)
    shrink = (inverse * lax.psum(partial_output, "tp")).astype(jnp.bfloat16)
    row_index = lax.axis_index("sp") * rows_here + jnp.arange(rows_here, dtype=jnp.int32)[:, None]
    member = (
        (row_index >= adapter_first_rows[None, :])
        & (row_index < (adapter_first_rows + adapter_row_counts)[None, :])
    ).astype(jnp.bfloat16)
    raised_gate = (member[:, :, None] * shrink[:, None, :rank_single]).reshape(
        rows_here, adapter_total * rank_single
    )
    raised_up = (member[:, :, None] * shrink[:, None, rank_single:]).reshape(
        rows_here, adapter_total * rank_single
    )
    column_slice = adapter_up_maps.shape[3]
    gate_output = gate_base + jnp.dot(
        raised_gate,
        adapter_up_maps[0].reshape(adapter_total * rank_single, column_slice),
        preferred_element_type=jnp.float32,
    )
    up_output = up_base + jnp.dot(
        raised_up,
        adapter_up_maps[1].reshape(adapter_total * rank_single, column_slice),
        preferred_element_type=jnp.float32,
    )
    return (jax.nn.silu(gate_output) * up_output).astype(jnp.bfloat16)


SLOTS = 4


def ring_kernel(
    n, ranks, adapters,
    tokens, gain, first, count, gate_w, up_w, down, raise_maps,
    out,
    own, held, acc, weights, down_v, raise_v, tokens_v, gain_v, first_s, count_s,
    squares, part, sums, sums_in, total_sums, raised, inverse,
    ring_send, ring_recv, sum_send, sum_recv, weight_sem, map_sem,
):
    rows, width = tokens.shape
    half = width // 2
    units = out.shape[1]
    last = n - 1
    levels = n.bit_length() - 1
    me = lax.axis_index("tp")
    side = me % 2
    place = me // 2 + side * (n - 1 - 2 * (me // 2))

    def device_at(p):
        upper = p // (n // 2)
        return (1 - upper) * 2 * p + upper * (2 * (n - 1 - p) + 1)

    sends_to = (device_at((place + 1) % n), device_at((place + n - 1) % n))

    def owner_of(d, k):
        distance = k // 2 + 1
        return device_at((place + n - distance) % n) if d == 0 else device_at((place + distance) % n)

    def half_of(d, k):
        return k % 2 if d == 0 else 1 - k % 2

    quarter = rows // 4
    pieces = ((0, 2 * quarter), (2 * quarter, quarter), (3 * quarter, quarter))

    def ring_copy(d, k, src):
        return pltpu.make_async_remote_copy(
            src_ref=src, dst_ref=held.at[d, k],
            send_sem=ring_send.at[d, k], recv_sem=ring_recv.at[d, k],
            device_id={"tp": sends_to[d]}, device_id_type=MESH,
        )

    def piece_copy(d, p):
        here = pl.ds(*pieces[p])
        return pltpu.make_async_remote_copy(
            src_ref=held.at[d, last - 3, here], dst_ref=held.at[d, last - 1, here],
            send_sem=ring_send.at[d, last - 1 + p], recv_sem=ring_recv.at[d, last - 1 + p],
            device_id={"tp": sends_to[d]}, device_id_type=MESH,
        )

    def sum_copy(level):
        step = 2 ** (level % levels)
        partner = me + step * (1 - 2 * ((me // step) % 2))
        if level == 0:
            src, dst = part.at[1 - side], sums_in.at[0]
        elif level < levels:
            src, dst = sums.at[level - 1], sums_in.at[level]
        else:
            src, dst = sums.at[level - 1], total_sums.at[side]
        return pltpu.make_async_remote_copy(
            src_ref=src, dst_ref=dst,
            send_sem=sum_send.at[level], recv_sem=sum_recv.at[level],
            device_id={"tp": partner}, device_id_type=MESH,
        )

    def weight_copies(slot, start):
        here = pl.ds(pl.multiple_of(start, half), half)
        return (
            pltpu.make_async_copy(gate_w.at[here, :], weights.at[slot, 0], weight_sem.at[slot, 0]),
            pltpu.make_async_copy(up_w.at[here, :], weights.at[slot, 1], weight_sem.at[slot, 1]),
        )

    def fetch(slot, start):
        for c in weight_copies(slot, start):
            c.start()

    def fetched(slot):
        for c in weight_copies(slot, 0):
            c.wait()

    def start_of(d, k):
        return owner_of(d, k) * width + half_of(d, k) * half

    barrier = pltpu.get_barrier_semaphore()
    for d in range(1, n):
        pl.semaphore_signal(barrier, inc=1, device_id={"tp": (me + d) % n}, device_id_type=MESH)

    down_copy = pltpu.make_async_copy(down, down_v, map_sem.at[0])
    raise_copy = pltpu.make_async_copy(raise_maps, raise_v, map_sem.at[1])
    tokens_copy = pltpu.make_async_copy(tokens, tokens_v, map_sem.at[2])
    gain_copy = pltpu.make_async_copy(gain, gain_v, map_sem.at[3])
    first_copy = pltpu.make_async_copy(first, first_s, map_sem.at[4])
    count_copy = pltpu.make_async_copy(count, count_s, map_sem.at[5])
    tokens_copy.start()
    gain_copy.start()
    first_copy.start()
    count_copy.start()
    down_copy.start()
    fetch(0, me * width)
    fetch(1, me * width + half)
    raise_copy.start()
    fetch(2, start_of(0, 0))

    gain_copy.wait()
    tokens_copy.wait()
    gain_row = gain_v[...].astype(F32).reshape(1, width)
    scale_rows = 64

    @pl.loop(0, rows // scale_rows)
    def _(i):
        here = pl.ds(pl.multiple_of(i * scale_rows, scale_rows), scale_rows)
        values = tokens_v[here, :].astype(F32)
        scaled = (values * gain_row).astype(BF16)
        own[0, here, :] = scaled[:, :half]
        own[1, here, :] = scaled[:, half:]
        squared = values * values
        total = squared[:, :128]
        for j in range(1, width // 128):
            total = total + squared[:, j * 128:(j + 1) * 128]
        squares[here, :] = total

    pl.semaphore_wait(barrier, n - 1)
    for k in range(2):
        for d in range(2):
            ring_copy(d, k, own.at[half_of(d, k)]).start()

    row_index = lax.broadcasted_iota(jnp.int32, (1, rows), 1) + lax.axis_index("sp") * rows

    def member(a):
        return (row_index >= first_s[a]) & (row_index < first_s[a] + count_s[a])

    first_copy.wait()
    count_copy.wait()
    down_copy.wait()
    middle = rows // 2
    part[...] = jnp.zeros(part.shape, F32)
    group = 4

    @pl.loop(0, adapters // group)
    def _(i):
        here = pl.ds(pl.multiple_of(i * group * ranks, group * ranks), group * ranks)
        dims = (((1,), (1,)), ((), ()))
        terms = lax.dot_general(down_v[here, :half], own[0], dims, preferred_element_type=F32)
        terms = terms + lax.dot_general(down_v[here, half:], own[1], dims, preferred_element_type=F32)
        total = jnp.zeros((ranks, rows), F32)
        for j in range(group):
            total = total + jnp.where(member(i * group + j), terms[j * ranks:(j + 1) * ranks, :], 0.0)
        part[0, 0:ranks, :] += total[:, :middle]
        part[1, 0:ranks, :] += total[:, middle:]

    square_sum = jnp.sum(jnp.transpose(squares[...]), axis=0, keepdims=True)
    square_sums = jnp.broadcast_to(square_sum, (8, rows))
    part[0, ranks:ranks + 8, :] = square_sums[:, :middle]
    part[1, ranks:ranks + 8, :] = square_sums[:, middle:]
    sum_copy(0).start()

    tile = 512 if units % 512 == 0 else units

    def product(x, slot, w, here):
        return jnp.dot(x, weights[slot, w, :, here], preferred_element_type=F32)

    def tiles(body):
        @pl.loop(0, units // tile)
        def _(i):
            body(pl.ds(pl.multiple_of(i * tile, tile), tile))

    fetched(0)
    fetch(3, start_of(1, 0))
    fetched(1)

    def own_tile(here):
        for w in range(2):
            acc[w, :, here] = product(own[0], 0, w, here) + product(own[1], 1, w, here)

    tiles(own_tile)

    def arrive(k):
        for d in range(2):
            ring_copy(d, k, own.at[0]).wait_recv()

            @pl.when(k + 3 < last)
            def _():
                ring_copy(d, k + 2, held.at[d, k]).start()

            @pl.when(k + 3 == last)
            def _():
                for p in range(len(pieces)):
                    piece_copy(d, p).start()

    def slots_of(k):
        low = 2 * ((k + 1) % 2)
        return low, low + 1

    def prefetch(k):
        @pl.when(k + 1 < last)
        def _():
            low, high = slots_of(k + 1)
            fetch(low, start_of(0, k + 1))
            fetch(high, start_of(1, k + 1))

    def steps(low, high, scaled):
        def step(k, carry):
            prefetch(k)
            arrive(k)
            s0, s1 = slots_of(k)
            fetched(s0)
            fetched(s1)

            def body(here):
                for w in range(2):
                    term = product(held[0, k], s0, w, here) + product(held[1, k], s1, w, here)
                    if scaled:
                        term = term * inverse[:, 0:1]
                    acc[w, :, here] += term

            tiles(body)
            return carry

        lax.fori_loop(low, high, step, 0)

    for level in range(levels):
        steps(level, level + 1, False)
        sum_copy(level).wait()
        sums[level] = (part[side] if level == 0 else sums[level - 1]) + sums_in[level]
        sum_copy(level + 1).start()
    total_sums[side] = sums[levels - 1]
    steps(levels, levels + 1, False)
    sum_copy(levels).wait()

    found_sums = jnp.concatenate([total_sums[0], total_sums[1]], axis=1)
    inverse_row = lax.rsqrt(found_sums[ranks:ranks + 1, :] / (width * n) + epsilon)
    shrink = (found_sums[0:ranks, :] * inverse_row).astype(BF16).astype(F32)
    inverse[...] = jnp.transpose(jnp.broadcast_to(inverse_row, (128, rows)))
    rank = ranks // 2

    for a in range(adapters):
        chosen = jnp.where(member(a), shrink, 0.0).astype(BF16)
        for w in range(2):
            raised[w, a * rank:(a + 1) * rank, :] = chosen[w * rank:(w + 1) * rank, :]
    raise_copy.wait()
    depth = adapters * rank

    def raise_tile(here):
        for w in range(2):
            term = lax.dot_general(
                raised[w], raise_v[w * depth:(w + 1) * depth, here],
                (((0,), (0,)), ((), ())), preferred_element_type=F32,
            )
            acc[w, :, here] = acc[w, :, here] * inverse[:, 0:1] + term

    tiles(raise_tile)

    steps(levels + 1, last - 1, True)

    s0, s1 = slots_of(last - 1)
    fetched(s0)
    fetched(s1)

    for p, (low, size) in enumerate(pieces):
        for d in range(2):
            piece_copy(d, p).wait_recv()
        those = pl.ds(low, size)

        def final_tile(here):
            found = []
            for w in range(2):
                term = product(held[0, last - 1, those], s0, w, here)
                term = term + product(held[1, last - 1, those], s1, w, here)
                found.append(acc[w, those, here] + term * inverse[those, 0:1])
            gate, up = found
            out[those, here] = (gate / (1.0 + jnp.exp(-gate)) * up).astype(out.dtype)

        tiles(final_tile)

    for d in range(2):
        for k in range(last - 1):
            ring_copy(d, k, own.at[0]).wait_send()
        for p in range(len(pieces)):
            piece_copy(d, p).wait_send()


def local_ring(
    n, tokens, norm_gain_vector, gate_weight, up_weight, adapter_down_maps, adapter_up_maps,
    adapter_of_row, adapter_first_rows, adapter_row_counts,
):
    rows, width = tokens.shape
    units = gate_weight.shape[1]
    adapters, _, ranks = adapter_down_maps.shape
    half = width // 2
    levels = n.bit_length() - 1
    down = jnp.transpose(adapter_down_maps, (0, 2, 1)).reshape(adapters * ranks, width)
    raise_maps = adapter_up_maps.reshape(adapters * ranks, units)
    vmem = pl.BlockSpec(memory_space=pltpu.VMEM)
    hbm = pl.BlockSpec(memory_space=pltpu.HBM)
    dma = pltpu.SemaphoreType.DMA
    return pl.pallas_call(
        functools.partial(ring_kernel, n, ranks, adapters),
        out_shape=jax.ShapeDtypeStruct((rows, units), BF16),
        in_specs=[hbm] * 8,
        out_specs=vmem,
        scratch_shapes=[
            pltpu.VMEM((2, rows, half), BF16),
            pltpu.VMEM((2, n - 1, rows, half), BF16),
            pltpu.VMEM((2, rows, units), F32),
            pltpu.VMEM((SLOTS, 2, half, units), BF16),
            pltpu.VMEM((adapters * ranks, width), BF16),
            pltpu.VMEM((adapters * ranks, units), BF16),
            pltpu.VMEM((rows, width), BF16),
            pltpu.VMEM(norm_gain_vector.shape, BF16),
            pltpu.SMEM(adapter_first_rows.shape, jnp.int32),
            pltpu.SMEM(adapter_row_counts.shape, jnp.int32),
            pltpu.VMEM((rows, 128), F32),
            pltpu.VMEM((2, ranks + 8, rows // 2), F32),
            pltpu.VMEM((levels, ranks + 8, rows // 2), F32),
            pltpu.VMEM((levels, ranks + 8, rows // 2), F32),
            pltpu.VMEM((2, ranks + 8, rows // 2), F32),
            pltpu.VMEM((2, adapters * ranks // 2, rows), BF16),
            pltpu.VMEM((rows, 128), F32),
            dma((2, n + 1)),
            dma((2, n + 1)),
            dma((levels + 1,)),
            dma((levels + 1,)),
            dma((SLOTS, 2)),
            dma((6,)),
        ],
        compiler_params=pltpu.CompilerParams(
            collective_id=0, has_side_effects=True, vmem_limit_bytes=60 * 1024 * 1024
        ),
        cost_estimate=pl.CostEstimate(
            flops=4 * rows * width * n * units, bytes_accessed=4 * width * n * units,
            transcendentals=rows * units,
        ),
    )(
        tokens, norm_gain_vector, adapter_first_rows, adapter_row_counts,
        gate_weight, up_weight, down, raise_maps,
    )


def solution(mesh):
    placed = (
        P(("rep", "sp"), "tp"),
        P("tp"),
        P(None, "tp"),
        P(None, "tp"),
        P(None, "tp", None),
        P(None, None, None, "tp"),
        P(("rep", "sp")),
        P("rep"),
        P("rep"),
    )
    n = mesh.shape["tp"]

    def body(tokens, *others):
        ring = n % 2 == 0 and n & (n - 1) == 0 and 8 <= n <= 16 and tokens.shape[1] % 256 == 0
        if ring:
            return local_ring(n, tokens, *others)
        return local(tokens, *others)

    return jax.shard_map(
        body, mesh=mesh, in_specs=placed, out_specs=P(("rep", "sp"), "tp"), check_vma=False
    )
```

```python
import functools
import jax
import jax.numpy as jnp
from jax import lax
from jax.experimental import pallas as pl
from jax.experimental.pallas import tpu as pltpu
from jax.sharding import PartitionSpec as P

epsilon = 1e-05
MESH = pl.DeviceIdType.MESH
F32 = jnp.float32
BF16 = jnp.bfloat16


def rank_products(scaled_columns, adapter_slice, adapter_of_row):
    adapter_total, slice_width, rank_doubled = adapter_slice.shape
    adapter_flattened = jnp.transpose(adapter_slice, (1, 0, 2)).reshape(
        slice_width, adapter_total * rank_doubled
    )
    combined_terms = jnp.dot(scaled_columns, adapter_flattened, preferred_element_type=jnp.float32)
    combined_terms = combined_terms.reshape(scaled_columns.shape[0], adapter_total, rank_doubled)
    adapter_range = jnp.arange(adapter_total, dtype=jnp.int32)
    selector = (adapter_of_row[:, None] == adapter_range[None, :]).astype(jnp.float32)
    return jnp.sum(selector[:, :, None] * combined_terms, axis=1)


def local(
    tokens,
    norm_gain_vector,
    gate_weight,
    up_weight,
    adapter_down_maps,
    adapter_up_maps,
    adapter_of_row,
    adapter_first_rows,
    adapter_row_counts,
):
    rows_here = tokens.shape[0]
    total_width = tokens.shape[1] * lax.axis_size("tp")
    rank_single = adapter_up_maps.shape[2]
    adapter_total = adapter_up_maps.shape[1]
    values = tokens.astype(jnp.float32)
    gain_local = norm_gain_vector.astype(jnp.float32)
    scaled_input = (values * gain_local).astype(jnp.bfloat16)
    gathered, gain_all = (
        lax.all_gather(tokens, "tp", axis=1, tiled=True),
        lax.all_gather(norm_gain_vector, "tp", axis=0, tiled=True),
    )
    wide_values = gathered.astype(jnp.float32)
    inverse = lax.rsqrt(
        jnp.sum(wide_values * wide_values, axis=1, keepdims=True) / total_width + epsilon
    )
    normed_input = (wide_values * inverse * gain_all.astype(jnp.float32)).astype(jnp.bfloat16)
    gate_base = jnp.dot(normed_input, gate_weight, preferred_element_type=jnp.float32)
    up_base = jnp.dot(normed_input, up_weight, preferred_element_type=jnp.float32)
    partial_output = rank_products(scaled_input, adapter_down_maps, adapter_of_row)
    shrink = (inverse * lax.psum(partial_output, "tp")).astype(jnp.bfloat16)
    row_index = lax.axis_index("sp") * rows_here + jnp.arange(rows_here, dtype=jnp.int32)[:, None]
    member = (
        (row_index >= adapter_first_rows[None, :])
        & (row_index < (adapter_first_rows + adapter_row_counts)[None, :])
    ).astype(jnp.bfloat16)
    raised_gate = (member[:, :, None] * shrink[:, None, :rank_single]).reshape(
        rows_here, adapter_total * rank_single
    )
    raised_up = (member[:, :, None] * shrink[:, None, rank_single:]).reshape(
        rows_here, adapter_total * rank_single
    )
    column_slice = adapter_up_maps.shape[3]
    gate_output = gate_base + jnp.dot(
        raised_gate,
        adapter_up_maps[0].reshape(adapter_total * rank_single, column_slice),
        preferred_element_type=jnp.float32,
    )
    up_output = up_base + jnp.dot(
        raised_up,
        adapter_up_maps[1].reshape(adapter_total * rank_single, column_slice),
        preferred_element_type=jnp.float32,
    )
    return (jax.nn.silu(gate_output) * up_output).astype(jnp.bfloat16)


SLOTS = 4


def ring_kernel(
    n, ranks, adapters,
    tokens, gain, first, count, gate_w, up_w, down, raise_maps,
    result,
    out, own, held, acc, weights, down_v, raise_v, tokens_v, gain_v, first_s, count_s,
    squares, part, sums, sums_in, total_sums, raised, inverse,
    ring_send, ring_recv, sum_send, sum_recv, weight_sem, map_sem, out_sem,
):
    rows, width = tokens.shape
    half = width // 2
    units = out.shape[1]
    last = n - 1
    levels = n.bit_length() - 1
    me = lax.axis_index("tp")
    side = me % 2
    place = me // 2 + side * (n - 1 - 2 * (me // 2))

    def device_at(p):
        upper = p // (n // 2)
        return (1 - upper) * 2 * p + upper * (2 * (n - 1 - p) + 1)

    sends_to = (device_at((place + 1) % n), device_at((place + n - 1) % n))

    def owner_of(d, k):
        distance = k // 2 + 1
        return device_at((place + n - distance) % n) if d == 0 else device_at((place + distance) % n)

    def half_of(d, k):
        return k % 2 if d == 0 else 1 - k % 2

    quarter = rows // 4
    pieces = ((0, 2 * quarter), (2 * quarter, quarter), (3 * quarter, quarter))

    def ring_copy(d, k, src):
        return pltpu.make_async_remote_copy(
            src_ref=src, dst_ref=held.at[d, k],
            send_sem=ring_send.at[d, k], recv_sem=ring_recv.at[d, k],
            device_id={"tp": sends_to[d]}, device_id_type=MESH,
        )

    def result_copy(p):
        here = pl.ds(*pieces[p])
        return pltpu.make_async_copy(out.at[here], result.at[here], out_sem.at[p])

    def piece_copy(d, p):
        here = pl.ds(*pieces[p])
        return pltpu.make_async_remote_copy(
            src_ref=held.at[d, last - 3, here], dst_ref=held.at[d, last - 1, here],
            send_sem=ring_send.at[d, last - 1 + p], recv_sem=ring_recv.at[d, last - 1 + p],
            device_id={"tp": sends_to[d]}, device_id_type=MESH,
        )

    def partner_of(level):
        step = 2 ** level
        return me + step * (1 - 2 * ((me // step) % 2))

    def sum_copy(level):
        partner = partner_of(level % levels)
        if level == 0:
            src, dst = part.at[1 - side], sums_in.at[0]
        elif level < levels:
            src, dst = sums.at[level - 1], sums_in.at[level]
        else:
            src, dst = sums.at[level - 1], total_sums.at[side]
        return pltpu.make_async_remote_copy(
            src_ref=src, dst_ref=dst,
            send_sem=sum_send.at[level], recv_sem=sum_recv.at[level],
            device_id={"tp": partner}, device_id_type=MESH,
        )

    def weight_copies(slot, start):
        here = pl.ds(pl.multiple_of(start, half), half)
        return (
            pltpu.make_async_copy(gate_w.at[here, :], weights.at[slot, 0], weight_sem.at[slot, 0]),
            pltpu.make_async_copy(up_w.at[here, :], weights.at[slot, 1], weight_sem.at[slot, 1]),
        )

    def fetch(slot, start):
        for c in weight_copies(slot, start):
            c.start()

    def fetched(slot):
        for c in weight_copies(slot, 0):
            c.wait()

    def start_of(d, k):
        return owner_of(d, k) * width + half_of(d, k) * half

    barrier = pltpu.get_barrier_semaphore()
    greeted = [sends_to[0], sends_to[1], partner_of(0)] + [partner_of(l) for l in range(2, levels)]
    for other in greeted:
        pl.semaphore_signal(barrier, inc=1, device_id={"tp": other}, device_id_type=MESH)

    down_copy = pltpu.make_async_copy(down, down_v, map_sem.at[0])
    raise_copy = pltpu.make_async_copy(raise_maps, raise_v, map_sem.at[1])
    tokens_copy = pltpu.make_async_copy(tokens, tokens_v, map_sem.at[2])
    gain_copy = pltpu.make_async_copy(gain, gain_v, map_sem.at[3])
    first_copy = pltpu.make_async_copy(first, first_s, map_sem.at[4])
    count_copy = pltpu.make_async_copy(count, count_s, map_sem.at[5])
    tokens_copy.start()
    gain_copy.start()
    first_copy.start()
    count_copy.start()
    down_copy.start()
    fetch(0, me * width)
    fetch(1, me * width + half)
    raise_copy.start()
    fetch(2, start_of(0, 0))

    gain_copy.wait()
    tokens_copy.wait()
    gain_row = gain_v[...].astype(F32).reshape(1, width)
    scale_rows = 64

    @pl.loop(0, rows // scale_rows)
    def _(i):
        here = pl.ds(pl.multiple_of(i * scale_rows, scale_rows), scale_rows)
        values = tokens_v[here, :].astype(F32)
        scaled = (values * gain_row).astype(BF16)
        own[0, here, :] = scaled[:, :half]
        own[1, here, :] = scaled[:, half:]
        squared = values * values
        total = squared[:, :128]
        for j in range(1, width // 128):
            total = total + squared[:, j * 128:(j + 1) * 128]
        squares[here, :] = total

    pl.semaphore_wait(barrier, len(greeted))
    for k in range(2):
        for d in range(2):
            ring_copy(d, k, own.at[half_of(d, k)]).start()

    row_index = lax.broadcasted_iota(jnp.int32, (1, rows), 1) + lax.axis_index("sp") * rows

    def member(a):
        return (row_index >= first_s[a]) & (row_index < first_s[a] + count_s[a])

    first_copy.wait()
    count_copy.wait()
    down_copy.wait()
    middle = rows // 2
    part[...] = jnp.zeros(part.shape, F32)
    group = 4

    @pl.loop(0, adapters // group)
    def _(i):
        here = pl.ds(pl.multiple_of(i * group * ranks, group * ranks), group * ranks)
        dims = (((1,), (1,)), ((), ()))
        terms = lax.dot_general(down_v[here, :half], own[0], dims, preferred_element_type=F32)
        terms = terms + lax.dot_general(down_v[here, half:], own[1], dims, preferred_element_type=F32)
        total = jnp.zeros((ranks, rows), F32)
        for j in range(group):
            total = total + jnp.where(member(i * group + j), terms[j * ranks:(j + 1) * ranks, :], 0.0)
        part[0, 0:ranks, :] += total[:, :middle]
        part[1, 0:ranks, :] += total[:, middle:]

    square_sum = jnp.sum(jnp.transpose(squares[...]), axis=0, keepdims=True)
    square_sums = jnp.broadcast_to(square_sum, (8, rows))
    part[0, ranks:ranks + 8, :] = square_sums[:, :middle]
    part[1, ranks:ranks + 8, :] = square_sums[:, middle:]
    sum_copy(0).start()

    tile = 512 if units % 512 == 0 else units

    def product(x, slot, w, here):
        return jnp.dot(x, weights[slot, w, :, here], preferred_element_type=F32)

    def tiles(body):
        @pl.loop(0, units // tile)
        def _(i):
            body(pl.ds(pl.multiple_of(i * tile, tile), tile))

    fetched(0)
    fetch(3, start_of(1, 0))
    fetched(1)

    def own_tile(here):
        for w in range(2):
            acc[w, :, here] = product(own[0], 0, w, here) + product(own[1], 1, w, here)

    tiles(own_tile)

    def arrive(k):
        for d in range(2):
            ring_copy(d, k, own.at[0]).wait_recv()

            @pl.when(k + 3 < last)
            def _():
                ring_copy(d, k + 2, held.at[d, k]).start()

            @pl.when(k + 3 == last)
            def _():
                for p in range(len(pieces)):
                    piece_copy(d, p).start()

    def slots_of(k):
        low = 2 * ((k + 1) % 2)
        return low, low + 1

    def prefetch(k):
        @pl.when(k + 1 < last)
        def _():
            low, high = slots_of(k + 1)
            fetch(low, start_of(0, k + 1))
            fetch(high, start_of(1, k + 1))

    def steps(low, high, scaled):
        def step(k, carry):
            prefetch(k)
            arrive(k)
            s0, s1 = slots_of(k)
            fetched(s0)
            fetched(s1)

            def body(here):
                for w in range(2):
                    term = product(held[0, k], s0, w, here) + product(held[1, k], s1, w, here)
                    if scaled:
                        term = term * inverse[:, 0:1]
                    acc[w, :, here] += term

            tiles(body)
            return carry

        lax.fori_loop(low, high, step, 0)

    for level in range(levels):
        steps(level, level + 1, False)
        sum_copy(level).wait()
        sums[level] = (part[side] if level == 0 else sums[level - 1]) + sums_in[level]
        sum_copy(level + 1).start()
    total_sums[side] = sums[levels - 1]
    steps(levels, levels + 1, False)
    sum_copy(levels).wait()

    found_sums = jnp.concatenate([total_sums[0], total_sums[1]], axis=1)
    inverse_row = lax.rsqrt(found_sums[ranks:ranks + 1, :] / (width * n) + epsilon)
    shrink = (found_sums[0:ranks, :] * inverse_row).astype(BF16).astype(F32)
    inverse[...] = jnp.transpose(jnp.broadcast_to(inverse_row, (128, rows)))
    rank = ranks // 2

    for a in range(adapters):
        chosen = jnp.where(member(a), shrink, 0.0).astype(BF16)
        for w in range(2):
            raised[w, a * rank:(a + 1) * rank, :] = chosen[w * rank:(w + 1) * rank, :]
    raise_copy.wait()
    depth = adapters * rank

    def raise_tile(here):
        for w in range(2):
            term = lax.dot_general(
                raised[w], raise_v[w * depth:(w + 1) * depth, here],
                (((0,), (0,)), ((), ())), preferred_element_type=F32,
            )
            acc[w, :, here] = acc[w, :, here] * inverse[:, 0:1] + term

    tiles(raise_tile)

    steps(levels + 1, last - 1, True)

    s0, s1 = slots_of(last - 1)
    fetched(s0)
    fetched(s1)

    for p, (low, size) in enumerate(pieces):
        for d in range(2):
            piece_copy(d, p).wait_recv()
        those = pl.ds(low, size)

        def final_tile(here):
            found = []
            for w in range(2):
                term = product(held[0, last - 1, those], s0, w, here)
                term = term + product(held[1, last - 1, those], s1, w, here)
                found.append(acc[w, those, here] + term * inverse[those, 0:1])
            gate, up = found
            out[those, here] = (gate / (1.0 + jnp.exp(-gate)) * up).astype(out.dtype)

        tiles(final_tile)
        result_copy(p).start()

    for p in range(len(pieces)):
        result_copy(p).wait()
    for d in range(2):
        for k in range(last - 1):
            ring_copy(d, k, own.at[0]).wait_send()
        for p in range(len(pieces)):
            piece_copy(d, p).wait_send()


def local_ring(
    n, tokens, norm_gain_vector, gate_weight, up_weight, adapter_down_maps, adapter_up_maps,
    adapter_of_row, adapter_first_rows, adapter_row_counts,
):
    rows, width = tokens.shape
    units = gate_weight.shape[1]
    adapters, _, ranks = adapter_down_maps.shape
    half = width // 2
    levels = n.bit_length() - 1
    down = jnp.transpose(adapter_down_maps, (0, 2, 1)).reshape(adapters * ranks, width)
    raise_maps = adapter_up_maps.reshape(adapters * ranks, units)
    hbm = pl.BlockSpec(memory_space=pltpu.HBM)
    dma = pltpu.SemaphoreType.DMA
    return pl.pallas_call(
        functools.partial(ring_kernel, n, ranks, adapters),
        out_shape=jax.ShapeDtypeStruct((rows, units), BF16),
        in_specs=[hbm] * 8,
        out_specs=hbm,
        scratch_shapes=[
            pltpu.VMEM((rows, units), BF16),
            pltpu.VMEM((2, rows, half), BF16),
            pltpu.VMEM((2, n - 1, rows, half), BF16),
            pltpu.VMEM((2, rows, units), F32),
            pltpu.VMEM((SLOTS, 2, half, units), BF16),
            pltpu.VMEM((adapters * ranks, width), BF16),
            pltpu.VMEM((adapters * ranks, units), BF16),
            pltpu.VMEM((rows, width), BF16),
            pltpu.VMEM(norm_gain_vector.shape, BF16),
            pltpu.SMEM(adapter_first_rows.shape, jnp.int32),
            pltpu.SMEM(adapter_row_counts.shape, jnp.int32),
            pltpu.VMEM((rows, 128), F32),
            pltpu.VMEM((2, ranks + 8, rows // 2), F32),
            pltpu.VMEM((levels, ranks + 8, rows // 2), F32),
            pltpu.VMEM((levels, ranks + 8, rows // 2), F32),
            pltpu.VMEM((2, ranks + 8, rows // 2), F32),
            pltpu.VMEM((2, adapters * ranks // 2, rows), BF16),
            pltpu.VMEM((rows, 128), F32),
            dma((2, n + 1)),
            dma((2, n + 1)),
            dma((levels + 1,)),
            dma((levels + 1,)),
            dma((SLOTS, 2)),
            dma((6,)),
            dma((3,)),
        ],
        compiler_params=pltpu.CompilerParams(
            collective_id=0, has_side_effects=True, vmem_limit_bytes=60 * 1024 * 1024
        ),
        cost_estimate=pl.CostEstimate(
            flops=4 * rows * width * n * units, bytes_accessed=4 * width * n * units,
            transcendentals=rows * units,
        ),
    )(
        tokens, norm_gain_vector, adapter_first_rows, adapter_row_counts,
        gate_weight, up_weight, down, raise_maps,
    )


def solution(mesh):
    placed = (
        P(("rep", "sp"), "tp"),
        P("tp"),
        P(None, "tp"),
        P(None, "tp"),
        P(None, "tp", None),
        P(None, None, None, "tp"),
        P(("rep", "sp")),
        P("rep"),
        P("rep"),
    )
    n = mesh.shape["tp"]

    def body(tokens, *others):
        ring = n % 2 == 0 and n & (n - 1) == 0 and 8 <= n <= 16 and tokens.shape[1] % 256 == 0
        if ring:
            return local_ring(n, tokens, *others)
        return local(tokens, *others)

    return jax.shard_map(
        body, mesh=mesh, in_specs=placed, out_specs=P(("rep", "sp"), "tp"), check_vma=False
    )
```
